128 devices in a mesh: batch: 128 (over y, x, z, core).
Axes of the slice: x: 4, y: 4, z: 4, core: 2. Of those that a mesh axis runs over, the one named last changes fastest.
Arguments:
- features: bfloat16 [131072, 1024], P('batch'), may hold values from -24 to 24
- head: bfloat16 [1024, 256], replicated, may hold values from -0.1875 to 0.1875
- partner: int32 [131072], P('batch'), may hold values from 0 to 131071, as said below
Outputs:
- feature_grad: bfloat16 [131072, 1024], P('batch')
- head_grad: float32 [1024, 256], P('batch')
The draws below stay inside these ranges and needn't reach their ends.
Inputs may be any that keep to these rules, and one draw needn't show every extreme that they name: `partner`: partner_i differs from i and lies in a block 1 to 4 blocks away from i's block, circularly.
All inputs are finite; a program needn't handle non-finite values.
Results may differ from the reference program's by a relative error of at most 0.0058.
Values may be sent and summed in bfloat16 or wider, within the bound.
No kernel may reach another device: no remote copies, remote signals or barrier semaphores. Data moves between devices by JAX's collectives and lax.ppermute only.
A program may use at most 64 MiB of HBM per device.

```python
import jax
import jax.numpy as jnp
from jax import lax

H = 1024
E = 256
ROWS = 1024
ROUNDS = 4
TOTAL = 131072
N_BATCH = 128


def draw_partner(key, part):
    key = jax.random.fold_in(key, 5)
    key_mag, key_side, key_row = jax.random.split(key, 3)
    ids = jnp.arange(TOTAL, dtype=jnp.int32)
    block = ids // ROWS
    magnitude = jax.random.randint(key_mag, (TOTAL,), 1, ROUNDS + 1, dtype=jnp.int32)
    side = jax.random.randint(key_side, (TOTAL,), 0, 2, dtype=jnp.int32) * 2 - 1
    target = (block + magnitude * side) % N_BATCH
    row = jax.random.randint(key_row, (TOTAL,), 0, ROWS, dtype=jnp.int32)
    chosen = target * ROWS + row
    chosen = chosen.at[0].set(TOTAL - 1)
    chosen = chosen.at[TOTAL - 1].set(0)
    return chosen.astype(jnp.int32)


def raised(drawn, own_key, source, target, shards_of, factor):
    def block_of(axis_at):
        return (jnp.arange(drawn.shape[axis_at]) // (drawn.shape[axis_at] // shards_of)).reshape((-1,) + (1,) * (drawn.ndim - 1 - axis_at))

    first = jax.random.permutation(own_key, shards_of)[block_of(target)]
    other_side = (block_of(target) + shards_of // 2) % shards_of
    return jnp.where((block_of(source) == first) | (block_of(source) == other_side), factor * drawn, drawn)


def level_of(own_key, extent, pieces, low, largest):
    def one(axis_at, shards_of):
        steps = jax.random.uniform(jax.random.fold_in(jax.random.fold_in(own_key, 6), axis_at), (shards_of,), jnp.float32, low / len(pieces), largest / len(pieces))
        return jnp.repeat(jnp.exp(steps), extent[axis_at] // shards_of).reshape((-1,) + (1,) * (len(extent) - axis_at - 1))

    loudness = one(*pieces[0])
    for cut in pieces[1:]:
        loudness = loudness * one(*cut)
    return loudness


def normal_values(stream_key, dims, width, reach, cuts=(), kind=jnp.bfloat16):
    values = jax.random.normal(stream_key, dims, jnp.float32) * width
    if len(cuts) > 0:
        values = level_of(stream_key, dims, cuts, -0.22, 0.18) * values
    return jnp.clip(values, min=-reach, max=reach).astype(kind)


def heavy_noise(rng, extent, spread, bound, cuts, heavy, kind=jnp.bfloat16):
    result = spread * jax.random.normal(rng, extent, jnp.float32)
    if cuts:
        result = result * level_of(rng, extent, cuts, -0.22, 0.18)
    return jnp.clip(raised(result, jax.random.fold_in(rng, 3), *heavy), -bound, bound).astype(kind)


def setup_inputs(seed: int = 0) -> dict:
    seeds = jax.random.split(jax.random.key(seed), 4)
    return {
        "features": heavy_noise(seeds[0], (TOTAL, H), 1.0, 24.0, ((0, 128),), (0, 1, 128, 5.5)),
        "head": normal_values(seeds[1], (H, E), H ** -0.5, 0.1875),
        "partner": draw_partner(jax.random.fold_in(seeds[3], 71), 0),
    }


def tile_coef(z_a, ids_a, part_a, z_b, ids_b, part_b, total):
    scores = jnp.dot(z_a, z_b.T, preferred_element_type=jnp.float32)
    positive = (part_a[:, None] == ids_b[None, :]) | (part_b[None, :] == ids_a[:, None])
    signs = jnp.where(positive, 1.0, -1.0).astype(jnp.float32)
    logits = 10.0 * scores - 10.0
    coef = -signs * jax.nn.sigmoid(-signs * logits) * (20.0 / total)
    return jnp.where(ids_a[:, None] != ids_b[None, :], coef, 0.0).astype(jnp.bfloat16)

def reference(features, head, partner):
    raw = jnp.dot(features, head, preferred_element_type=jnp.float32)
    scale = lax.rsqrt(lax.optimization_barrier(jnp.sum(raw * raw, axis=1, keepdims=True)) + 1e-06)
    unit = raw * scale
    embed = unit.astype(jnp.bfloat16)
    ids = jnp.arange(TOTAL, dtype=jnp.int32)
    block_z = embed.reshape(N_BATCH, ROWS, E)
    block_p = partner.reshape(N_BATCH, ROWS)
    block_i = ids.reshape(N_BATCH, ROWS)

    def one_block(owner):
        grad = jnp.zeros((ROWS, E), jnp.float32)
        for offset in range(-ROUNDS, ROUNDS + 1):
            other = ((owner + offset) % N_BATCH).astype(jnp.int32)
            coef = tile_coef(block_z[owner], block_i[owner], block_p[owner], block_z[other], block_i[other], block_p[other], float(TOTAL))
            term = jnp.dot(coef, block_z[other], preferred_element_type=jnp.float32)
            if offset > 0:
                term = lax.optimization_barrier(term.astype(jnp.bfloat16)).astype(jnp.float32)
            grad = grad + term
        return grad
    embed_grad = lax.map(one_block, jnp.arange(N_BATCH, dtype=jnp.int32)).reshape(TOTAL, E)
    raw_grad = ((embed_grad - unit * lax.optimization_barrier(jnp.sum(unit * embed_grad, axis=1, keepdims=True))) * scale).astype(jnp.bfloat16)
    feature_grad = jnp.dot(raw_grad, head.T, preferred_element_type=jnp.float32).astype(jnp.bfloat16)
    head_grad = jnp.dot(features.T, raw_grad, preferred_element_type=jnp.float32)
    return (feature_grad, head_grad)
```

```python
import jax
import jax.numpy as jnp
from jax import lax
from jax.sharding import PartitionSpec as P

ROUNDS = 4


def passed_along(x, axis, by):
    size = lax.axis_size(axis)
    return lax.ppermute(x, axis, [(i, (i + by) % size) for i in range(size)])


def tile_coef(z_a, ids_a, part_a, z_b, ids_b, part_b, total):
    scores = jnp.dot(z_a, z_b.T, preferred_element_type=jnp.float32)
    positive = (part_a[:, None] == ids_b[None, :]) | (part_b[None, :] == ids_a[:, None])
    signs = jnp.where(positive, 1.0, -1.0).astype(jnp.float32)
    logits = 10.0 * scores - 10.0
    coef = -signs * jax.nn.sigmoid(-signs * logits) * (20.0 / total)
    return jnp.where(ids_a[:, None] != ids_b[None, :], coef, 0.0).astype(jnp.bfloat16)


def per_device(features, head, partner):
    rows = features.shape[0]
    count = lax.axis_size("batch")
    owner = lax.axis_index("batch")
    total = float(rows * count)
    raw = jnp.dot(features, head, preferred_element_type=jnp.float32)
    scale = lax.rsqrt(jnp.sum(raw * raw, axis=1, keepdims=True) + 1e-06)
    unit = raw * scale
    embed = unit.astype(jnp.bfloat16)
    local = jnp.arange(rows, dtype=jnp.int32)
    my_ids = owner * rows + local
    coef = tile_coef(embed, my_ids, partner, embed, my_ids, partner, total)
    grad = jnp.dot(coef, embed, preferred_element_type=jnp.float32)
    for step in range(1, ROUNDS + 1):
        other_z, other_p = passed_along((embed, partner), "batch", step)
        other_ids = (owner - step) % count * rows + local
        coef = tile_coef(embed, my_ids, partner, other_z, other_ids, other_p, total)
        grad = grad + jnp.dot(coef, other_z, preferred_element_type=jnp.float32)
        backward = jnp.dot(coef.T, embed, preferred_element_type=jnp.float32).astype(jnp.bfloat16)
        returned = passed_along(backward, "batch", -step)
        grad = grad + returned.astype(jnp.float32)
    raw_grad = ((grad - unit * jnp.sum(unit * grad, axis=1, keepdims=True)) * scale).astype(
        jnp.bfloat16
    )
    feature_grad = jnp.dot(raw_grad, head.T, preferred_element_type=jnp.float32).astype(
        jnp.bfloat16
    )
    partial = lax.dot_general(
        features, raw_grad, (((0,), (0,)), ((), ())), preferred_element_type=jnp.float32
    ).astype(jnp.bfloat16)
    parts = lax.all_to_all(partial.reshape(count, -1, partial.shape[1]), "batch", 0, 0)
    head_grad = jnp.sum(parts.astype(jnp.float32), axis=0)
    return (feature_grad, head_grad)


def solution(mesh):
    in_specs = (P("batch", None), P(), P("batch"))
    out_specs = (P("batch", None), P("batch", None))
    return jax.shard_map(
        per_device, mesh=mesh, in_specs=in_specs, out_specs=out_specs, check_vma=False
    )
```

```python
import functools
import math

import jax
import jax.numpy as jnp
from jax import lax
from jax.experimental import pallas as pl
from jax.experimental.pallas import tpu as pltpu
from jax.sharding import PartitionSpec as P

BF16, F32 = jnp.bfloat16, jnp.float32
ROWS, E, CODE = 1024, 256, 16
TILE = 256
VMEM = pl.BlockSpec(memory_space=pltpu.VMEM)
SMEM = pl.BlockSpec(memory_space=pltpu.SMEM)
BOTH_LAST = (((1,), (1,)), ((), ()))
BOTH_FIRST = (((0,), (0,)), ((), ()))
LIMIT = 24 * 2**20


def call(body, outs, specs, flops, aliases=None):
    return pl.pallas_call(
        body,
        out_shape=outs,
        in_specs=specs,
        out_specs=jax.tree.map(lambda _: VMEM, outs),
        input_output_aliases=aliases or {},
        compiler_params=pltpu.CompilerParams(vmem_limit_bytes=LIMIT),
        cost_estimate=pl.CostEstimate(flops=flops, bytes_accessed=4 * 2**20, transcendentals=0),
    )


def partners(msg_ref):
    code = msg_ref[ROWS : ROWS + CODE, :].astype(F32)
    return code[0:4, :] * 512.0 + code[4:8, :]


def across(rows):
    return jnp.concatenate([rows[k : k + 1, :] for k in range(4)], axis=1)


def embed_kernel(features_ref, head_ref, partner_ref, msg_ref, raw_ref):
    step = pl.program_id(0)
    raw = jnp.dot(features_ref[...], head_ref[...], preferred_element_type=F32)
    scale = lax.rsqrt(jnp.sum(raw * raw, axis=1, keepdims=True) + 1e-06)
    raw_ref[...] = raw
    at = pl.multiple_of(step * TILE, TILE)
    msg_ref[pl.ds(at, TILE), :] = (raw * scale).astype(BF16)

    @pl.when(step == 0)
    def _():
        ids = partner_ref[...]
        high = (ids + 256) >> 9
        low = ids - (high << 9)
        code = jnp.concatenate([high, low, jnp.zeros((8, E), jnp.int32)], axis=0)
        msg_ref[ROWS : ROWS + CODE, :] = code.astype(F32).astype(BF16)


def embed(features, head, partner):
    return pl.pallas_call(
        embed_kernel,
        grid=(ROWS // TILE,),
        out_shape=(
            jax.ShapeDtypeStruct((ROWS + CODE, E), BF16),
            jax.ShapeDtypeStruct((ROWS, E), F32),
        ),
        in_specs=[
            pl.BlockSpec((TILE, features.shape[1]), lambda i: (i, 0)),
            pl.BlockSpec(head.shape, lambda i: (0, 0)),
            pl.BlockSpec((4, E), lambda i: (0, 0)),
        ],
        out_specs=(
            pl.BlockSpec((ROWS + CODE, E), lambda i: (0, 0)),
            pl.BlockSpec((TILE, E), lambda i: (i, 0)),
        ),
        compiler_params=pltpu.CompilerParams(vmem_limit_bytes=LIMIT),
        cost_estimate=pl.CostEstimate(
            flops=2 * ROWS * 1024 * E, bytes_accessed=4 * 2**20, transcendentals=0
        ),
    )(features, head, partner.reshape(4, E))


def term(rows_ref, cols_ref, total, found, same=False):
    weight = 20.0 / total
    slope = 10.0 * math.log2(math.e)
    shift = slope - math.log2(weight)
    cols = cols_ref[0:ROWS, :]
    for at in range(0, ROWS, TILE):
        tile = slice(at, at + TILE)
        scores = lax.dot_general(rows_ref[tile, :], cols, BOTH_LAST, preferred_element_type=F32)
        coef = 1.0 / (jnp.exp2(shift - scores * slope) + 1.0 / weight)
        if same:
            i = lax.broadcasted_iota(jnp.int32, (TILE, ROWS), 0) + at
            j = lax.broadcasted_iota(jnp.int32, (TILE, ROWS), 1)
            coef = jnp.where(i != j, coef, 0.0)
        else:
            coef = jnp.where(found(at), coef - weight, coef)
        yield tile, jnp.dot(coef.astype(BF16), cols, preferred_element_type=F32)


def matcher(row_partner_ref, row_base, row_block, col_partner, col_block):
    j = lax.broadcasted_iota(jnp.int32, (1, ROWS), 1) + col_block * ROWS
    col_ids = j.astype(F32)

    def found(at):
        i = lax.broadcasted_iota(jnp.int32, (TILE, 1), 0) + (row_block * ROWS + at)
        row_ids = i.astype(F32)
        theirs = row_partner_ref[row_base + at : row_base + at + TILE, :]
        return (jnp.tile(theirs, (1, ROWS // 128)) == col_ids) | (col_partner == row_ids)

    return found


def diagonal_kernel(total, mine_ref, grad_ref):
    for tile, value in term(mine_ref, mine_ref, total, None, same=True):
        grad_ref[tile, :] = value


def chip_kernel(total, block_ref, mine_ref, other_ref, grad_ref, new_ref, spread_ref):
    for base, ref in ((0, mine_ref), (ROWS, other_ref)):
        ids = partners(ref)
        for k in range(8):
            piece = ids[k // 2 : k // 2 + 1, (k % 2) * 128 : (k % 2) * 128 + 128]
            spread_ref[base + k * 128 : base + k * 128 + 128, :] = jnp.broadcast_to(
                piece, (128, 128)
            ).T
    found = matcher(spread_ref, 0, block_ref[0], across(partners(other_ref)), block_ref[1])
    for tile, value in term(mine_ref, other_ref, total, found):
        new_ref[tile, :] = grad_ref[tile, :] + value


def mine_kernel(total, which, block_ref, cols_ref, mine_ref, spread_ref, grad_ref, new_ref):
    found = matcher(
        spread_ref, 0, block_ref[0], across(partners(cols_ref)), block_ref[which]
    )
    for tile, value in term(mine_ref, cols_ref, total, found):
        new_ref[tile, :] = grad_ref[tile, :] + value


def other_kernel(total, which, start, block_ref, cols_ref, other_ref, spread_ref, *rest):
    new_ref = rest[-1]
    found = matcher(
        spread_ref, ROWS, block_ref[1], across(partners(cols_ref)), block_ref[which]
    )
    for tile, value in term(other_ref, cols_ref, total, found):
        if not start:
            value = rest[0][tile, :] + value
        new_ref[tile, :] = value.astype(new_ref.dtype)


def final_kernel(features_ref, raw_ref, grad_ref, extra_ref, raw_grad_ref, partial_ref):
    raw = raw_ref[...]
    grad = grad_ref[...] + extra_ref[...].astype(F32)
    scale = lax.rsqrt(jnp.sum(raw * raw, axis=1, keepdims=True) + 1e-06)
    unit = raw * scale
    along = jnp.sum(unit * grad, axis=1, keepdims=True)
    raw_grad_ref[...] = ((grad - unit * along) * scale).astype(BF16)
    partial_ref[...] = lax.dot_general(
        features_ref[...], raw_grad_ref[...], BOTH_FIRST, preferred_element_type=F32
    ).astype(BF16)


def feature_kernel(raw_grad_ref, head_ref, out_ref):
    out_ref[...] = lax.dot_general(
        raw_grad_ref[...], head_ref[...], BOTH_LAST, preferred_element_type=F32
    ).astype(BF16)


def per_device(features, head, partner):
    count = lax.axis_size("batch")
    owner = lax.axis_index("batch")
    total = float(ROWS * count)
    pair = 4 * ROWS * ROWS * E
    shape = jax.ShapeDtypeStruct
    full = shape((ROWS, E), F32)

    def across_chip(x):
        return lax.ppermute(x, "batch", [(i, i ^ 1) for i in range(count)])

    def onward(x):
        hops = [(i, (i + (2 if i % 2 == 0 else -2)) % count) for i in range(count)]
        return lax.ppermute(x, "batch", hops)

    core = owner % 2
    chip = owner // 2
    back = jnp.where(core == 0, -1, 1)
    near = (chip + back) % (count // 2)
    far = (chip + 2 * back) % (count // 2)
    blocks = jnp.stack(
        [
            owner,
            owner ^ 1,
            2 * near + core,
            2 * near + 1 - core,
            2 * far + core,
            2 * far + 1 - core,
        ]
    ).astype(jnp.int32)

    mine, raw = embed(features, head, partner)
    near_same = onward(mine)
    other = across_chip(mine)
    near_cross = onward(other)
    far_same = onward(near_same)
    far_cross = onward(near_cross)

    grad = call(functools.partial(diagonal_kernel, total), full, [VMEM], pair)(mine)
    grad, spread = call(
        functools.partial(chip_kernel, total),
        (full, shape((2 * ROWS, 128), F32)),
        [SMEM, VMEM, VMEM, VMEM],
        pair,
    )(blocks, mine, other, grad)

    def on_mine(grad, which, cols):
        return call(
            functools.partial(mine_kernel, total, which), full, [SMEM] + [VMEM] * 4, pair
        )(blocks, cols, mine, spread, grad)

    def on_other(grad, which, cols, out=full):
        given = () if grad is None else (grad,)
        return call(
            functools.partial(other_kernel, total, which, grad is None),
            out,
            [SMEM] + [VMEM] * (3 + len(given)),
            pair,
        )(blocks, cols, other, spread, *given)

    theirs = on_other(None, 2, near_same)
    grad = on_mine(grad, 2, near_same)
    theirs = on_other(theirs, 3, near_cross)
    grad = on_mine(grad, 3, near_cross)
    grad = on_mine(grad, 4, far_same)
    theirs = on_other(theirs, 5, far_cross, shape((ROWS, E), BF16))
    extra = across_chip(theirs)
    grad = on_mine(grad, 5, far_cross)

    raw_grad, partial = call(
        final_kernel,
        (shape((ROWS, E), BF16), shape((features.shape[1], E), BF16)),
        [VMEM] * 4,
        pair // 2,
    )(features, raw, grad, extra)
    parts = lax.all_to_all(partial.reshape(count, -1, E), "batch", 0, 0)
    feature_grad = call(
        feature_kernel, shape((ROWS, features.shape[1]), BF16), [VMEM] * 2, pair // 2
    )(raw_grad, head)
    head_grad = jnp.sum(parts.astype(F32), axis=0)
    return (feature_grad, head_grad)


def solution(mesh):
    in_specs = (P("batch", None), P(), P("batch"))
    out_specs = (P("batch", None), P("batch", None))
    return jax.shard_map(
        per_device, mesh=mesh, in_specs=in_specs, out_specs=out_specs, check_vma=False
    )
```

```python
import functools
import math

import jax
import jax.numpy as jnp
from jax import lax
from jax.experimental import pallas as pl
from jax.experimental.pallas import tpu as pltpu
from jax.sharding import PartitionSpec as P

BF16, F32 = jnp.bfloat16, jnp.float32
ROWS, E, CODE = 1024, 256, 16
TILE = 256
VMEM = pl.BlockSpec(memory_space=pltpu.VMEM)
ANY = pl.BlockSpec(memory_space=pl.ANY)
SMEM = pl.BlockSpec(memory_space=pltpu.SMEM)
BOTH_LAST = (((1,), (1,)), ((), ()))
BOTH_FIRST = (((0,), (0,)), ((), ()))
LIMIT = 24 * 2**20
EMBED_LIMIT = 60 * 2**20
COST = 3


def call(body, outs, specs, flops, aliases=None):
    return pl.pallas_call(
        body,
        out_shape=outs,
        in_specs=specs,
        out_specs=jax.tree.map(lambda _: VMEM, outs) if not aliases else (VMEM, ANY),
        input_output_aliases=aliases or {},
        compiler_params=pltpu.CompilerParams(vmem_limit_bytes=LIMIT),
        cost_estimate=pl.CostEstimate(flops=int(COST * flops), bytes_accessed=4 * 2**20, transcendentals=0),
    )


def partners(msg_ref):
    code = msg_ref[ROWS : ROWS + CODE, :].astype(F32)
    return code[0:8, 0:128] * 512.0 + code[0:8, 128:256]


def across(rows):
    return jnp.concatenate([rows[k : k + 1, :] for k in range(8)], axis=1)


def embed_kernel(features_ref, head_ref, partner_ref, msg_ref, raw_ref, held, weights, arrived):
    tiles = [slice(at, at + TILE) for at in range(0, ROWS, TILE)]
    copies = [pltpu.make_async_copy(head_ref, weights, arrived.at[len(tiles)])]
    for k, tile in enumerate(tiles):
        copies.append(pltpu.make_async_copy(features_ref.at[tile, :], held.at[tile, :], arrived.at[k]))
    for copy in copies:
        copy.start()
    ids = partner_ref[...]
    high = (ids + 256) >> 9
    low = ids - (high << 9)
    code = jnp.concatenate([high, low], axis=1)
    code = jnp.concatenate([code, jnp.zeros((8, E), jnp.int32)], axis=0)
    msg_ref[ROWS : ROWS + CODE, :] = code.astype(F32).astype(BF16)
    copies[0].wait()
    for copy, tile in zip(copies[1:], tiles):
        copy.wait()
        raw = jnp.dot(held[tile, :], weights[...], preferred_element_type=F32)
        scale = lax.rsqrt(jnp.sum(raw * raw, axis=1, keepdims=True) + 1e-06)
        raw_ref[tile, :] = raw
        msg_ref[tile, :] = (raw * scale).astype(BF16)


def embed(features, head, partner):
    return pl.pallas_call(
        embed_kernel,
        out_shape=(
            jax.ShapeDtypeStruct((ROWS + CODE, E), BF16),
            jax.ShapeDtypeStruct((ROWS, E), F32),
        ),
        in_specs=[
            pl.BlockSpec(memory_space=pltpu.HBM),
            pl.BlockSpec(memory_space=pltpu.HBM),
            VMEM,
        ],
        out_specs=(VMEM, VMEM),
        scratch_shapes=[
            pltpu.VMEM(features.shape, BF16),
            pltpu.VMEM(head.shape, BF16),
            pltpu.SemaphoreType.DMA((ROWS // TILE + 1,)),
        ],
        compiler_params=pltpu.CompilerParams(vmem_limit_bytes=EMBED_LIMIT),
        cost_estimate=pl.CostEstimate(
            flops=2 * ROWS * 1024 * E, bytes_accessed=4 * 2**20, transcendentals=0
        ),
    )(features, head, partner.reshape(8, 128))


def term(rows_ref, cols_ref, total, found, same=False):
    weight = 20.0 / total
    slope = 10.0 * math.log2(math.e)
    shift = slope - math.log2(weight)
    cols = cols_ref[0:ROWS, :]
    for at in range(0, ROWS, TILE):
        tile = slice(at, at + TILE)
        scores = lax.dot_general(rows_ref[tile, :], cols, BOTH_LAST, preferred_element_type=F32)
        coef = 1.0 / (jnp.exp2(shift - scores * slope) + 1.0 / weight)
        if same:
            i = lax.broadcasted_iota(jnp.int32, (TILE, ROWS), 0) + at
            j = lax.broadcasted_iota(jnp.int32, (TILE, ROWS), 1)
            coef = jnp.where(i != j, coef, 0.0)
        else:
            coef = jnp.where(found(at), coef - weight, coef)
        yield tile, jnp.dot(coef.astype(BF16), cols, preferred_element_type=F32)


def matcher(row_partner_ref, row_base, row_block, col_partner, col_block):
    j = lax.broadcasted_iota(jnp.int32, (1, ROWS), 1) + col_block * ROWS
    col_ids = j.astype(F32)

    def found(at):
        i = lax.broadcasted_iota(jnp.int32, (TILE, 1), 0) + (row_block * ROWS + at)
        row_ids = i.astype(F32)
        theirs = row_partner_ref[row_base + at : row_base + at + TILE, :]
        return (jnp.tile(theirs, (1, ROWS // 128)) == col_ids) | (col_partner == row_ids)

    return found


def diagonal_kernel(total, mine_ref, grad_ref):
    for tile, value in term(mine_ref, mine_ref, total, None, same=True):
        grad_ref[tile, :] = value


def chip_kernel(total, block_ref, mine_ref, other_ref, grad_ref, new_ref, spread_ref):
    for base, ref in ((0, mine_ref), (ROWS, other_ref)):
        ids = partners(ref)
        for k in range(8):
            spread_ref[base + k * 128 : base + k * 128 + 128, :] = jnp.broadcast_to(
                ids[k : k + 1, :], (128, 128)
            ).T
    found = matcher(spread_ref, 0, block_ref[0], across(partners(other_ref)), block_ref[1])
    for tile, value in term(mine_ref, other_ref, total, found):
        new_ref[tile, :] = grad_ref[tile, :] + value


def rows_kernel(total, which, jobs, outs, block_ref, cols_ref, spread_ref, *refs):
    refs = list(refs)
    given = [(refs.pop(0), refs.pop(0) if summed else None) for _, summed in jobs]
    columns = across(partners(cols_ref))
    refs = refs[len(refs) - outs :]
    for (place, _), (rows_ref, old_ref), new_ref in zip(jobs, given, refs):
        found = matcher(spread_ref, place * ROWS, block_ref[place], columns, block_ref[which])
        for tile, value in term(rows_ref, cols_ref, total, found):
            if old_ref is not None:
                value = old_ref[tile, :].astype(F32) + value
            new_ref[tile, :] = value.astype(new_ref.dtype)


def final_kernel(features_ref, raw_ref, grad_ref, extra_ref, raw_grad_ref, partial_ref):
    raw = raw_ref[...]
    grad = grad_ref[...] + extra_ref[...].astype(F32)
    scale = lax.rsqrt(jnp.sum(raw * raw, axis=1, keepdims=True) + 1e-06)
    unit = raw * scale
    along = jnp.sum(unit * grad, axis=1, keepdims=True)
    raw_grad_ref[...] = ((grad - unit * along) * scale).astype(BF16)
    partial_ref[...] = lax.dot_general(
        features_ref[...], raw_grad_ref[...], BOTH_FIRST, preferred_element_type=F32
    ).astype(BF16)


def feature_kernel(raw_grad_ref, head_ref, out_ref):
    out_ref[...] = lax.dot_general(
        raw_grad_ref[...], head_ref[...], BOTH_LAST, preferred_element_type=F32
    ).astype(BF16)


def per_device(features, head, partner):
    count = lax.axis_size("batch")
    owner = lax.axis_index("batch")
    total = float(ROWS * count)
    pair = 4 * ROWS * ROWS * E
    shape = jax.ShapeDtypeStruct
    full = shape((ROWS, E), F32)

    def across_chip(x):
        return lax.ppermute(x, "batch", [(i, i ^ 1) for i in range(count)])

    def onward(x):
        hops = [(i, (i + (2 if i % 2 == 0 else -2)) % count) for i in range(count)]
        return lax.ppermute(x, "batch", hops)

    core = owner % 2
    chip = owner // 2
    back = jnp.where(core == 0, -1, 1)
    near = (chip + back) % (count // 2)
    far = (chip + 2 * back) % (count // 2)
    blocks = jnp.stack(
        [
            owner,
            owner ^ 1,
            2 * near + core,
            2 * near + 1 - core,
            2 * far + core,
            2 * far + 1 - core,
        ]
    ).astype(jnp.int32)

    mine, raw = embed(features, head, partner)
    near_same = onward(mine)
    other = across_chip(mine)
    near_cross = onward(other)
    far_same = onward(near_same)
    far_cross = onward(near_cross)

    grad = call(functools.partial(diagonal_kernel, total), full, [VMEM], pair)(mine)
    grad, spread = call(
        functools.partial(chip_kernel, total),
        (full, shape((2 * ROWS, 128), F32)),
        [SMEM, VMEM, VMEM, VMEM],
        pair,
    )(blocks, mine, other, grad)

    def on_rows(which, cols, jobs, outs, passed=None):
        given = [x for rows, old in jobs for x in ((rows,) if old is None else (rows, old))]
        plan = tuple((0 if rows is mine else 1, old is not None) for rows, old in jobs)
        return call(
            functools.partial(rows_kernel, total, which, plan, len(outs) + (passed is not None)),
            tuple(outs) + (() if passed is None else (shape(passed.shape, passed.dtype),)),
            [SMEM] + [VMEM] * (2 + len(given)) + ([] if passed is None else [ANY]),
            len(jobs) * pair,
            {} if passed is None else {3 + len(given): len(outs)},
        )(blocks, cols, spread, *given, *(() if passed is None else (passed,)))

    theirs, grad = on_rows(2, near_same, [(other, None), (mine, grad)], [full, full])
    theirs, grad = on_rows(3, near_cross, [(other, theirs), (mine, grad)], [full, full])
    grad, theirs = on_rows(4, far_same, [(mine, grad)], [full], theirs)
    (theirs,) = on_rows(5, far_cross, [(other, theirs)], [shape((ROWS, E), BF16)])
    extra = across_chip(theirs)
    (grad,) = on_rows(5, far_cross, [(mine, grad)], [full])

    raw_grad, partial = call(
        final_kernel,
        (shape((ROWS, E), BF16), shape((features.shape[1], E), BF16)),
        [VMEM] * 4,
        pair // 2,
    )(features, raw, grad, extra)
    parts = lax.all_to_all(partial.reshape(count, -1, E), "batch", 0, 0)
    feature_grad = call(
        feature_kernel, shape((ROWS, features.shape[1]), BF16), [VMEM] * 2, pair // 2
    )(raw_grad, head)
    head_grad = jnp.sum(parts.astype(F32), axis=0)
    return (feature_grad, head_grad)


def solution(mesh):
    in_specs = (P("batch", None), P(), P("batch"))
    out_specs = (P("batch", None), P("batch", None))
    return jax.shard_map(
        per_device, mesh=mesh, in_specs=in_specs, out_specs=out_specs, check_vma=False
    )
```

```python
import functools
import math

import jax
import jax.numpy as jnp
from jax import lax
from jax.experimental import pallas as pl
from jax.experimental.pallas import tpu as pltpu
from jax.sharding import PartitionSpec as P

BF16, F32 = jnp.bfloat16, jnp.float32
ROWS, E, CODE = 1024, 256, 16
TILE = 256
VMEM = pl.BlockSpec(memory_space=pltpu.VMEM)
ANY = pl.BlockSpec(memory_space=pl.ANY)
SMEM = pl.BlockSpec(memory_space=pltpu.SMEM)
BOTH_LAST = (((1,), (1,)), ((), ()))
BOTH_FIRST = (((0,), (0,)), ((), ()))
LIMIT = 24 * 2**20
EMBED_LIMIT = 60 * 2**20
COST = 6
EMBED_TILE = 1024
SAME_PARTS, CROSS_PARTS = 1, 2


def call(body, outs, specs, flops, aliases=None):
    return pl.pallas_call(
        body,
        out_shape=outs,
        in_specs=specs,
        out_specs=jax.tree.map(lambda _: VMEM, outs) if not aliases else (VMEM, ANY),
        input_output_aliases=aliases or {},
        compiler_params=pltpu.CompilerParams(vmem_limit_bytes=LIMIT),
        cost_estimate=pl.CostEstimate(flops=int(COST * flops), bytes_accessed=4 * 2**20, transcendentals=0),
    )


def partners(part_ref):
    size = part_ref.shape[0] - CODE
    code = part_ref[size : size + CODE, :].astype(F32)
    lines = size // 128
    return code[0:lines, 0:128] * 512.0 + code[0:lines, 128:256]


def embed_kernel(cuts, features_ref, head_ref, partner_ref, *refs):
    raw_ref, parts = refs[0], refs[1 : 1 + len(cuts)]
    held, weights, ids_held, raw_held, unit_held, code_held, arrived, left = refs[1 + len(cuts) :]
    tiles = [slice(at, at + EMBED_TILE) for at in range(0, ROWS, EMBED_TILE)]
    arrivals = [
        pltpu.make_async_copy(partner_ref, ids_held, arrived.at[len(tiles) + 1]),
        pltpu.make_async_copy(head_ref, weights, arrived.at[len(tiles)]),
    ]
    for k, tile in enumerate(tiles):
        arrivals.append(
            pltpu.make_async_copy(features_ref.at[tile, :], held.at[tile, :], arrived.at[k])
        )
    for copy in arrivals:
        copy.start()
    leavings = []

    def leave(source, target):
        copy = pltpu.make_async_copy(source, target, left.at[len(leavings)])
        copy.start()
        leavings.append(copy)

    arrivals[0].wait()
    ids = ids_held[...]
    high = (ids + 256) >> 9
    low = ids - (high << 9)
    code = jnp.concatenate([high, low], axis=1).astype(F32)
    for k, ((at, size), ref) in enumerate(zip(cuts, parts)):
        lines = code[at // 128 : (at + size) // 128, :]
        blank = jnp.zeros((CODE - size // 128, E), F32)
        code_held[k] = jnp.concatenate([lines, blank], axis=0).astype(BF16)
        leave(code_held.at[k], ref.at[size : size + CODE, :])
    arrivals[1].wait()
    for copy, tile in zip(arrivals[2:], tiles):
        copy.wait()
        raw = jnp.dot(held[tile, :], weights[...], preferred_element_type=F32)
        scale = lax.rsqrt(jnp.sum(raw * raw, axis=1, keepdims=True) + 1e-06)
        unit_held[tile, :] = (raw * scale).astype(BF16)
        for (at, size), ref in zip(cuts, parts):
            low_at, high_at = max(at, tile.start), min(at + size, tile.stop)
            if low_at < high_at:
                leave(unit_held.at[low_at:high_at, :], ref.at[low_at - at : high_at - at, :])
        raw_held[tile, :] = raw
        leave(raw_held.at[tile, :], raw_ref.at[tile, :])
    for copy in leavings:
        copy.wait()


def embed(features, head, partner, cuts):
    outs = [jax.ShapeDtypeStruct((ROWS, E), F32)]
    outs += [jax.ShapeDtypeStruct((size + CODE, E), BF16) for _, size in cuts]
    hbm = pl.BlockSpec(memory_space=pltpu.HBM)
    tiles = ROWS // EMBED_TILE
    held = sum(max(size // EMBED_TILE, 1) for _, size in cuts)
    return pl.pallas_call(
        functools.partial(embed_kernel, cuts),
        out_shape=outs,
        in_specs=[hbm, hbm, hbm],
        out_specs=[hbm] * len(outs),
        scratch_shapes=[
            pltpu.VMEM(features.shape, BF16),
            pltpu.VMEM(head.shape, BF16),
            pltpu.VMEM((8, 128), jnp.int32),
            pltpu.VMEM((ROWS, E), F32),
            pltpu.VMEM((ROWS, E), BF16),
            pltpu.VMEM((len(cuts), CODE, E), BF16),
            pltpu.SemaphoreType.DMA((tiles + 2,)),
            pltpu.SemaphoreType.DMA((len(cuts) + held + tiles,)),
        ],
        compiler_params=pltpu.CompilerParams(vmem_limit_bytes=EMBED_LIMIT),
        cost_estimate=pl.CostEstimate(
            flops=2 * ROWS * 1024 * E, bytes_accessed=4 * 2**20, transcendentals=0
        ),
    )(features, head, partner.reshape(8, 128))


def tile_of(parts, at):
    size = parts[0].shape[0] - CODE
    return parts[at // size][at % size : at % size + TILE, :]


def term(rows, cols_ref, total, found, same_at=None):
    weight = 20.0 / total
    slope = 10.0 * math.log2(math.e)
    shift = slope - math.log2(weight)
    size = cols_ref.shape[0] - CODE
    cols = cols_ref[0:size, :]
    for at in range(0, ROWS, TILE):
        scores = lax.dot_general(tile_of(rows, at), cols, BOTH_LAST, preferred_element_type=F32)
        coef = 1.0 / (jnp.exp2(shift - scores * slope) + 1.0 / weight)
        if same_at is not None:
            i = lax.broadcasted_iota(jnp.int32, (TILE, size), 0) + at
            j = lax.broadcasted_iota(jnp.int32, (TILE, size), 1) + same_at
            coef = jnp.where(i != j, coef, 0.0)
        else:
            coef = jnp.where(found(at), coef - weight, coef)
        yield slice(at, at + TILE), jnp.dot(coef.astype(BF16), cols, preferred_element_type=F32)


def matcher(spread_ref, place, row_block, cols_ref, col_block, col_at):
    ids = partners(cols_ref)
    col_partner = jnp.concatenate([ids[k : k + 1, :] for k in range(ids.shape[0])], axis=1)
    size = col_partner.shape[1]
    j = lax.broadcasted_iota(jnp.int32, (1, size), 1) + (col_block * ROWS + col_at)
    col_ids = j.astype(F32)

    def found(at):
        i = lax.broadcasted_iota(jnp.int32, (TILE, 1), 0) + (row_block * ROWS + at)
        row_ids = i.astype(F32)
        theirs = spread_ref[place * ROWS + at : place * ROWS + at + TILE, :]
        return (jnp.tile(theirs, (1, size // 128)) == col_ids) | (col_partner == row_ids)

    return found


def diagonal_kernel(total, *refs):
    mine, grad_ref = refs[:-1], refs[-1]
    size = mine[0].shape[0] - CODE
    for k, part in enumerate(mine):
        for tile, value in term(mine, part, total, None, same_at=k * size):
            grad_ref[tile, :] = value if k == 0 else grad_ref[tile, :] + value


def chip_kernel(total, n_mine, block_ref, *refs):
    mine, other = refs[:n_mine], refs[n_mine:-3]
    grad_ref, new_ref, spread_ref = refs[-3:]
    for base, parts in ((0, mine), (ROWS, other)):
        at = base
        for part in parts:
            ids = partners(part)
            for k in range(ids.shape[0]):
                spread_ref[at : at + 128, :] = jnp.broadcast_to(ids[k : k + 1, :], (128, 128)).T
                at += 128
    size = other[0].shape[0] - CODE
    for k, part in enumerate(other):
        found = matcher(spread_ref, 0, block_ref[0], part, block_ref[1], k * size)
        old_ref = grad_ref if k == 0 else new_ref
        for tile, value in term(mine, part, total, found):
            new_ref[tile, :] = old_ref[tile, :] + value


def rows_kernel(total, which, col_at, jobs, outs, block_ref, cols_ref, spread_ref, *refs):
    refs = list(refs)
    news = refs[len(refs) - outs :]
    for (place, count, summed), new_ref in zip(jobs, news):
        rows, refs = refs[:count], refs[count:]
        old_ref = refs.pop(0) if summed else None
        found = matcher(spread_ref, place, block_ref[place], cols_ref, block_ref[which], col_at)
        for tile, value in term(rows, cols_ref, total, found):
            if old_ref is not None:
                value = old_ref[tile, :].astype(F32) + value
            new_ref[tile, :] = value.astype(new_ref.dtype)


def final_kernel(features_ref, raw_ref, grad_ref, extra_ref, raw_grad_ref, partial_ref):
    raw = raw_ref[...]
    grad = grad_ref[...] + extra_ref[...].astype(F32)
    scale = lax.rsqrt(jnp.sum(raw * raw, axis=1, keepdims=True) + 1e-06)
    unit = raw * scale
    along = jnp.sum(unit * grad, axis=1, keepdims=True)
    raw_grad_ref[...] = ((grad - unit * along) * scale).astype(BF16)
    partial_ref[...] = lax.dot_general(
        features_ref[...], raw_grad_ref[...], BOTH_FIRST, preferred_element_type=F32
    ).astype(BF16)


def feature_kernel(raw_grad_ref, head_ref, out_ref):
    out_ref[...] = lax.dot_general(
        raw_grad_ref[...], head_ref[...], BOTH_LAST, preferred_element_type=F32
    ).astype(BF16)


def per_device(features, head, partner):
    count = lax.axis_size("batch")
    owner = lax.axis_index("batch")
    total = float(ROWS * count)
    pair = 4 * ROWS * ROWS * E
    shape = jax.ShapeDtypeStruct
    full = shape((ROWS, E), F32)

    def across_chip(x):
        return lax.ppermute(x, "batch", [(i, i ^ 1) for i in range(count)])

    def onward(x):
        hops = [(i, (i + (2 if i % 2 == 0 else -2)) % count) for i in range(count)]
        return lax.ppermute(x, "batch", hops)

    core = owner % 2
    chip = owner // 2
    back = jnp.where(core == 0, -1, 1)
    near = (chip + back) % (count // 2)
    far = (chip + 2 * back) % (count // 2)
    blocks = jnp.stack(
        [
            owner,
            owner ^ 1,
            2 * near + core,
            2 * near + 1 - core,
            2 * far + core,
            2 * far + 1 - core,
        ]
    ).astype(jnp.int32)

    def cut(n):
        return [(k * ROWS // n, ROWS // n) for k in range(n)]

    if SAME_PARTS == CROSS_PARTS:
        raw, *mine = embed(features, head, partner, cut(SAME_PARTS))
        given_over = mine
    else:
        raw, *parts = embed(features, head, partner, cut(SAME_PARTS) + cut(CROSS_PARTS))
        mine, given_over = parts[:SAME_PARTS], parts[SAME_PARTS:]
    near_same = [onward(x) for x in mine]
    other = [across_chip(x) for x in given_over]

    grad = call(functools.partial(diagonal_kernel, total), full, [VMEM] * len(mine), pair)(*mine)
    grad, spread = call(
        functools.partial(chip_kernel, total, len(mine)),
        (full, shape((2 * ROWS, 128), F32)),
        [SMEM] + [VMEM] * (len(mine) + len(other) + 1),
        pair,
    )(blocks, *mine, *other, grad)
    near_cross = [onward(x) for x in other]
    far_same = [onward(x) for x in near_same]
    far_cross = [onward(x) for x in near_cross]

    def on_rows(which, at, cols, jobs, outs, passed=None):
        given, plan = [], []
        for rows, old in jobs:
            plan.append((0 if rows is mine else 1, len(rows), old is not None))
            given += list(rows) + ([] if old is None else [old])
        tied = [] if passed is None else [passed]
        return call(
            functools.partial(rows_kernel, total, which, at, tuple(plan), len(outs) + len(tied)),
            tuple(outs) + tuple(shape(x.shape, x.dtype) for x in tied),
            [SMEM] + [VMEM] * (2 + len(given)) + [ANY] * len(tied),
            len(jobs) * pair * (cols.shape[0] - CODE) // ROWS,
            {3 + len(given): len(outs)} if tied else {},
        )(blocks, cols, spread, *given, *tied)

    theirs = None
    for which, group in ((2, near_same), (3, near_cross)):
        for k, cols in enumerate(group):
            theirs, grad = on_rows(
                which, k * ROWS // len(group), cols, [(other, theirs), (mine, grad)], [full, full]
            )
    for k, cols in enumerate(far_same):
        grad, theirs = on_rows(4, k * ROWS // len(far_same), cols, [(mine, grad)], [full], theirs)
    for k, cols in enumerate(far_cross[:-1]):
        theirs, grad = on_rows(
            5, k * ROWS // len(far_cross), cols, [(other, theirs), (mine, grad)], [full, full]
        )
    last_at = ROWS - ROWS // len(far_cross)
    cols = far_cross[-1]
    (theirs,) = on_rows(5, last_at, cols, [(other, theirs)], [shape((ROWS, E), BF16)])
    extra = across_chip(theirs)
    (grad,) = on_rows(5, last_at, cols, [(mine, grad)], [full])

    raw_grad, partial = call(
        final_kernel,
        (shape((ROWS, E), BF16), shape((features.shape[1], E), BF16)),
        [VMEM] * 4,
        pair // 2,
    )(features, raw, grad, extra)
    parts = lax.all_to_all(partial.reshape(count, -1, E), "batch", 0, 0)
    feature_grad = call(
        feature_kernel, shape((ROWS, features.shape[1]), BF16), [VMEM] * 2, pair // 2
    )(raw_grad, head)
    head_grad = jnp.sum(parts.astype(F32), axis=0)
    return (feature_grad, head_grad)


def solution(mesh):
    in_specs = (P("batch", None), P(), P("batch"))
    out_specs = (P("batch", None), P("batch", None))
    return jax.shard_map(
        per_device, mesh=mesh, in_specs=in_specs, out_specs=out_specs, check_vma=False
    )
```

```python
import functools
import math

import jax
import jax.numpy as jnp
from jax import lax
from jax.experimental import pallas as pl
from jax.experimental.pallas import tpu as pltpu
from jax.sharding import PartitionSpec as P

BF16, F32 = jnp.bfloat16, jnp.float32
ROWS, E, CODE = 1024, 256, 16
TILE = 256
VMEM = pl.BlockSpec(memory_space=pltpu.VMEM)
ANY = pl.BlockSpec(memory_space=pl.ANY)
BOTH_LAST = (((1,), (1,)), ((), ()))
BOTH_FIRST = (((0,), (0,)), ((), ()))
LIMIT = 24 * 2**20
EMBED_LIMIT = 60 * 2**20
COST = 1
OWN_COST = 0.3
EMBED_TILE = 1024
SAME_PARTS, CROSS_PARTS = 2, 2
TIES = 1


def call(body, outs, specs, flops, aliases=None):
    return pl.pallas_call(
        body,
        out_shape=outs,
        in_specs=specs,
        out_specs=jax.tree.map(lambda _: VMEM, outs) if not aliases else (VMEM, ANY),
        input_output_aliases=aliases or {},
        compiler_params=pltpu.CompilerParams(vmem_limit_bytes=LIMIT),
        cost_estimate=pl.CostEstimate(flops=int(COST * flops), bytes_accessed=4 * 2**20, transcendentals=0),
    )


def partners(part_ref):
    size = part_ref.shape[0] - CODE
    code = part_ref[size : size + CODE, :].astype(F32)
    lines = size // 128
    return code[0:lines, 0:128] * 512.0 + code[0:lines, 128:256]


def embed_kernel(cuts, features_ref, head_ref, partner_ref, *refs):
    raw_ref, parts = refs[0], refs[1 : 1 + len(cuts)]
    held, weights, ids_held, raw_held, unit_held, code_held, arrived, left = refs[1 + len(cuts) :]
    tiles = [slice(at, at + EMBED_TILE) for at in range(0, ROWS, EMBED_TILE)]
    arrivals = [
        pltpu.make_async_copy(partner_ref, ids_held, arrived.at[len(tiles) + 1]),
        pltpu.make_async_copy(head_ref, weights, arrived.at[len(tiles)]),
    ]
    for k, tile in enumerate(tiles):
        arrivals.append(
            pltpu.make_async_copy(features_ref.at[tile, :], held.at[tile, :], arrived.at[k])
        )
    for copy in arrivals:
        copy.start()
    leavings = []

    def leave(source, target):
        copy = pltpu.make_async_copy(source, target, left.at[len(leavings)])
        copy.start()
        leavings.append(copy)

    arrivals[0].wait()
    ids = ids_held[...]
    high = (ids + 256) >> 9
    low = ids - (high << 9)
    code = jnp.concatenate([high, low], axis=1).astype(F32)
    for k, ((at, size), ref) in enumerate(zip(cuts, parts)):
        lines = code[at // 128 : (at + size) // 128, :]
        blank = jnp.zeros((CODE - size // 128, E), F32)
        code_held[k] = jnp.concatenate([lines, blank], axis=0).astype(BF16)
        leave(code_held.at[k], ref.at[size : size + CODE, :])
    arrivals[1].wait()
    for copy, tile in zip(arrivals[2:], tiles):
        copy.wait()
        raw = jnp.dot(held[tile, :], weights[...], preferred_element_type=F32)
        scale = lax.rsqrt(jnp.sum(raw * raw, axis=1, keepdims=True) + 1e-06)
        unit_held[tile, :] = (raw * scale).astype(BF16)
        for (at, size), ref in zip(cuts, parts):
            low_at, high_at = max(at, tile.start), min(at + size, tile.stop)
            if low_at < high_at:
                leave(unit_held.at[low_at:high_at, :], ref.at[low_at - at : high_at - at, :])
        raw_held[tile, :] = raw
        leave(raw_held.at[tile, :], raw_ref.at[tile, :])
    for copy in leavings:
        copy.wait()


def embed(features, head, partner, cuts):
    outs = [jax.ShapeDtypeStruct((ROWS, E), F32)]
    outs += [jax.ShapeDtypeStruct((size + CODE, E), BF16) for _, size in cuts]
    hbm = pl.BlockSpec(memory_space=pltpu.HBM)
    tiles = ROWS // EMBED_TILE
    held = sum(max(size // EMBED_TILE, 1) for _, size in cuts)
    return pl.pallas_call(
        functools.partial(embed_kernel, cuts),
        out_shape=outs,
        in_specs=[hbm, hbm, hbm],
        out_specs=[hbm] * len(outs),
        scratch_shapes=[
            pltpu.VMEM(features.shape, BF16),
            pltpu.VMEM(head.shape, BF16),
            pltpu.VMEM((8, 128), jnp.int32),
            pltpu.VMEM((ROWS, E), F32),
            pltpu.VMEM((ROWS, E), BF16),
            pltpu.VMEM((len(cuts), CODE, E), BF16),
            pltpu.SemaphoreType.DMA((tiles + 2,)),
            pltpu.SemaphoreType.DMA((len(cuts) + held + tiles,)),
        ],
        compiler_params=pltpu.CompilerParams(vmem_limit_bytes=EMBED_LIMIT),
        cost_estimate=pl.CostEstimate(
            flops=2 * ROWS * 1024 * E, bytes_accessed=4 * 2**20, transcendentals=0
        ),
    )(features, head, partner.reshape(8, 128))


def tile_of(parts, at):
    size = parts[0].shape[0] - CODE
    return parts[at // size][at % size : at % size + TILE, :]


def term(rows, cols_ref, total, found, same_at=None):
    weight = 20.0 / total
    slope = 10.0 * math.log2(math.e)
    shift = slope - math.log2(weight)
    size = cols_ref.shape[0] - CODE
    cols = cols_ref[0:size, :]
    for at in range(0, ROWS, TILE):
        scores = lax.dot_general(tile_of(rows, at), cols, BOTH_LAST, preferred_element_type=F32)
        coef = 1.0 / (jnp.exp2(shift - scores * slope) + 1.0 / weight)
        if same_at is not None:
            i = lax.broadcasted_iota(jnp.int32, (TILE, size), 0) + at
            j = lax.broadcasted_iota(jnp.int32, (TILE, size), 1) + same_at
            coef = jnp.where(i != j, coef, 0.0)
        else:
            coef = coef.astype(BF16)
            coef = jnp.where(found(at), coef - jnp.bfloat16(weight), coef)
        yield slice(at, at + TILE), jnp.dot(coef.astype(BF16), cols, preferred_element_type=F32)


def matcher(spread_ref, place, row_first, cols_ref, col_first, col_at):
    ids = partners(cols_ref)
    col_partner = jnp.concatenate([ids[k : k + 1, :] for k in range(ids.shape[0])], axis=1)
    size = col_partner.shape[1]
    wide = size // 128

    def small(local, end):
        return jnp.clip(local, -1.0, float(end)).astype(jnp.int32).astype(jnp.int16)

    col_partner = col_partner - jnp.tile(row_first, (1, wide))
    col_partner = small(jnp.broadcast_to(col_partner, (16, size)), ROWS)
    col_partner = jnp.tile(col_partner, (TILE // 16, 1))
    col_ids = lax.broadcasted_iota(jnp.int32, (16, size), 1).astype(jnp.int16)
    col_ids = jnp.tile(col_ids, (TILE // 16, 1))

    def found(at):
        row_ids = (lax.broadcasted_iota(jnp.int32, (TILE, 128), 0) + at).astype(jnp.int16)
        theirs = spread_ref[place * ROWS + at : place * ROWS + at + TILE, :]
        theirs = small(theirs - (col_first + float(col_at)), size)
        return (jnp.tile(theirs, (1, wide)) == col_ids) | (
            col_partner == jnp.tile(row_ids, (1, wide))
        )

    return found


def diagonal_kernel(total, *refs):
    mine, grad_ref = refs[:-1], refs[-1]
    size = mine[0].shape[0] - CODE
    for k, part in enumerate(mine):
        for tile, value in term(mine, part, total, None, same_at=k * size):
            grad_ref[tile, :] = value if k == 0 else grad_ref[tile, :] + value


def chip_kernel(total, n_mine, first_ref, *refs):
    mine, other = refs[:n_mine], refs[n_mine:-4]
    grad_ref, new_ref, spread_ref, again_ref = refs[-4:]
    again_ref[...] = other[-1][...]
    for base, parts in ((0, mine), (ROWS, other)):
        at = base
        for part in parts:
            ids = partners(part)
            for k in range(ids.shape[0]):
                spread_ref[at : at + 128, :] = jnp.broadcast_to(ids[k : k + 1, :], (128, 128)).T
                at += 128
    size = other[0].shape[0] - CODE
    for k, part in enumerate(other):
        found = matcher(spread_ref, 0, first_ref[0:1, :], part, first_ref[1:2, :], k * size)
        old_ref = grad_ref if k == 0 else new_ref
        for tile, value in term(mine, part, total, found):
            new_ref[tile, :] = old_ref[tile, :] + value


def rows_kernel(total, which, col_at, jobs, outs, first_ref, cols_ref, spread_ref, *refs):
    refs = list(refs)
    news = refs[len(refs) - outs :]
    for (place, count, summed), new_ref in zip(jobs, news):
        rows, refs = refs[:count], refs[count:]
        old_ref = refs.pop(0) if summed else None
        row_first, col_first = first_ref[place : place + 1, :], first_ref[which : which + 1, :]
        found = matcher(spread_ref, place, row_first, cols_ref, col_first, col_at)
        for tile, value in term(rows, cols_ref, total, found):
            if old_ref is not None:
                value = old_ref[tile, :].astype(F32) + value
            new_ref[tile, :] = value.astype(new_ref.dtype)


def final_kernel(features_ref, raw_ref, grad_ref, extra_ref, raw_grad_ref, partial_ref):
    raw = raw_ref[...]
    grad = grad_ref[...] + extra_ref[...].astype(F32)
    scale = lax.rsqrt(jnp.sum(raw * raw, axis=1, keepdims=True) + 1e-06)
    unit = raw * scale
    along = jnp.sum(unit * grad, axis=1, keepdims=True)
    raw_grad_ref[...] = ((grad - unit * along) * scale).astype(BF16)
    partial_ref[...] = lax.dot_general(
        features_ref[...], raw_grad_ref[...], BOTH_FIRST, preferred_element_type=F32
    ).astype(BF16)


def feature_kernel(raw_grad_ref, head_ref, out_ref):
    out_ref[...] = lax.dot_general(
        raw_grad_ref[...], head_ref[...], BOTH_LAST, preferred_element_type=F32
    ).astype(BF16)


def per_device(features, head, partner):
    count = lax.axis_size("batch")
    owner = lax.axis_index("batch")
    total = float(ROWS * count)
    pair = 4 * ROWS * ROWS * E
    shape = jax.ShapeDtypeStruct
    full = shape((ROWS, E), F32)

    def across_chip(x):
        return lax.ppermute(x, "batch", [(i, i ^ 1) for i in range(count)])

    def onward(x):
        hops = [(i, (i + (2 if i % 2 == 0 else -2)) % count) for i in range(count)]
        return lax.ppermute(x, "batch", hops)

    core = owner % 2
    chip = owner // 2
    back = jnp.where(core == 0, -1, 1)
    near = (chip + back) % (count // 2)
    far = (chip + 2 * back) % (count // 2)
    first_ids = jnp.stack(
        [
            owner,
            owner ^ 1,
            2 * near + core,
            2 * near + 1 - core,
            2 * far + core,
            2 * far + 1 - core,
            owner,
            owner,
        ]
    )
    first_ids = jnp.broadcast_to((first_ids * ROWS).astype(F32)[:, None], (8, 128))

    def cut(n):
        return [(k * ROWS // n, ROWS // n) for k in range(n)]

    if SAME_PARTS == CROSS_PARTS:
        raw, *mine = embed(features, head, partner, cut(SAME_PARTS))
        given_over = mine
    else:
        raw, *parts = embed(features, head, partner, cut(SAME_PARTS) + cut(CROSS_PARTS))
        mine, given_over = parts[:SAME_PARTS], parts[SAME_PARTS:]
    near_same = [onward(x) for x in mine]
    other = [across_chip(x) for x in given_over]

    grad = call(functools.partial(diagonal_kernel, total), full, [VMEM] * len(mine), OWN_COST * pair)(*mine)
    grad, spread, again = call(
        functools.partial(chip_kernel, total, len(mine)),
        (full, shape((2 * ROWS, 128), F32), shape(other[-1].shape, BF16)),
        [VMEM] + [VMEM] * (len(mine) + len(other) + 1),
        OWN_COST * pair,
    )(first_ids, *mine, *other, grad)
    near_cross = [onward(x) for x in other[:-1] + [again]]
    far_same = [onward(x) for x in near_same]
    far_cross = [onward(x) for x in near_cross]

    def on_rows(which, at, cols, jobs, outs, passed=None, after=()):
        given, plan = [], []
        for rows, old in jobs:
            plan.append((0 if rows is mine else 1, len(rows), old is not None))
            given += list(rows) + ([] if old is None else [old])
        tied = [] if passed is None else [passed]
        return call(
            functools.partial(rows_kernel, total, which, at, tuple(plan), len(outs) + len(tied)),
            tuple(outs) + tuple(shape(x.shape, x.dtype) for x in tied),
            [VMEM] + [VMEM] * (2 + len(given)) + [ANY] * (len(tied) + len(after)),
            len(jobs) * pair * (cols.shape[0] - CODE) // ROWS,
            {3 + len(given): len(outs)} if tied else {},
        )(first_ids, cols, spread, *given, *tied, *after)

    theirs = None
    near = [(2, k * ROWS // len(near_same), x) for k, x in enumerate(near_same)]
    near += [(3, k * ROWS // len(near_cross), x) for k, x in enumerate(near_cross)]
    for k, (which, at, cols) in enumerate(near):
        after = [x for _, _, x in near[k + 1 : k + 2]] if k >= TIES else []
        theirs, grad = on_rows(
            which, at, cols, [(other, theirs), (mine, grad)], [full, full], after=after
        )
    for k, cols in enumerate(far_same):
        grad, theirs = on_rows(4, k * ROWS // len(far_same), cols, [(mine, grad)], [full], theirs)
    for k, cols in enumerate(far_cross[:-1]):
        theirs, grad = on_rows(
            5, k * ROWS // len(far_cross), cols, [(other, theirs), (mine, grad)], [full, full]
        )
    last_at = ROWS - ROWS // len(far_cross)
    cols = far_cross[-1]
    (theirs,) = on_rows(5, last_at, cols, [(other, theirs)], [shape((ROWS, E), BF16)])
    extra = across_chip(theirs)
    (grad,) = on_rows(5, last_at, cols, [(mine, grad)], [full])

    raw_grad, partial = call(
        final_kernel,
        (shape((ROWS, E), BF16), shape((features.shape[1], E), BF16)),
        [VMEM] * 4,
        pair // 2,
    )(features, raw, grad, extra)
    parts = lax.all_to_all(partial.reshape(count, -1, E), "batch", 0, 0)
    feature_grad = call(
        feature_kernel, shape((ROWS, features.shape[1]), BF16), [VMEM] * 2, pair // 2
    )(raw_grad, head)
    head_grad = jnp.sum(parts.astype(F32), axis=0)
    return (feature_grad, head_grad)


def solution(mesh):
    in_specs = (P("batch", None), P(), P("batch"))
    out_specs = (P("batch", None), P("batch", None))
    return jax.shard_map(
        per_device, mesh=mesh, in_specs=in_specs, out_specs=out_specs, check_vma=False
    )
```

```python
import functools
import math

import jax
import jax.numpy as jnp
from jax import lax
from jax.experimental import pallas as pl
from jax.experimental.pallas import tpu as pltpu
from jax.sharding import PartitionSpec as P

BF16, F32 = jnp.bfloat16, jnp.float32
ROWS, E, CODE = 1024, 256, 16
TILE = 256
FINAL_TILE = 512
VMEM = pl.BlockSpec(memory_space=pltpu.VMEM)
ANY = pl.BlockSpec(memory_space=pl.ANY)
BOTH_LAST = (((1,), (1,)), ((), ()))
BOTH_FIRST = (((0,), (0,)), ((), ()))
LIMIT = 24 * 2**20
EMBED_LIMIT = 60 * 2**20
COST = 0.7
OWN_COST = 0.3
EMBED_TILE = 1024
SAME_PARTS, CROSS_PARTS = 2, 2
TIES = 1


def call(body, outs, specs, flops, aliases=None):
    return pl.pallas_call(
        body,
        out_shape=outs,
        in_specs=specs,
        out_specs=jax.tree.map(lambda _: VMEM, outs) if not aliases else (VMEM, ANY),
        input_output_aliases=aliases or {},
        compiler_params=pltpu.CompilerParams(vmem_limit_bytes=LIMIT),
        cost_estimate=pl.CostEstimate(flops=int(COST * flops), bytes_accessed=4 * 2**20, transcendentals=0),
    )


def partners(part_ref):
    size = part_ref.shape[0] - CODE
    code = part_ref[size : size + CODE, :].astype(F32)
    lines = size // 128
    return code[0:lines, 0:128] * 512.0 + code[0:lines, 128:256]


def embed_kernel(cuts, features_ref, head_ref, partner_ref, *refs):
    raw_ref, parts = refs[0], refs[1 : 1 + len(cuts)]
    held, weights, ids_held, raw_held, unit_held, code_held, arrived, left = refs[1 + len(cuts) :]
    tiles = [slice(at, at + EMBED_TILE) for at in range(0, ROWS, EMBED_TILE)]
    arrivals = [
        pltpu.make_async_copy(partner_ref, ids_held, arrived.at[len(tiles) + 1]),
        pltpu.make_async_copy(head_ref, weights, arrived.at[len(tiles)]),
    ]
    for k, tile in enumerate(tiles):
        arrivals.append(
            pltpu.make_async_copy(features_ref.at[tile, :], held.at[tile, :], arrived.at[k])
        )
    for copy in arrivals:
        copy.start()
    leavings = []

    def leave(source, target):
        copy = pltpu.make_async_copy(source, target, left.at[len(leavings)])
        copy.start()
        leavings.append(copy)

    arrivals[0].wait()
    ids = ids_held[...]
    high = (ids + 256) >> 9
    low = ids - (high << 9)
    code = jnp.concatenate([high, low], axis=1).astype(F32)
    for k, ((at, size), ref) in enumerate(zip(cuts, parts)):
        lines = code[at // 128 : (at + size) // 128, :]
        blank = jnp.zeros((CODE - size // 128, E), F32)
        code_held[k] = jnp.concatenate([lines, blank], axis=0).astype(BF16)
        leave(code_held.at[k], ref.at[size : size + CODE, :])
    arrivals[1].wait()
    for copy, tile in zip(arrivals[2:], tiles):
        copy.wait()
        raw = jnp.dot(held[tile, :], weights[...], preferred_element_type=F32)
        scale = lax.rsqrt(jnp.sum(raw * raw, axis=1, keepdims=True) + 1e-06)
        unit_held[tile, :] = (raw * scale).astype(BF16)
        for (at, size), ref in zip(cuts, parts):
            low_at, high_at = max(at, tile.start), min(at + size, tile.stop)
            if low_at < high_at:
                leave(unit_held.at[low_at:high_at, :], ref.at[low_at - at : high_at - at, :])
        raw_held[tile, :] = raw
        leave(raw_held.at[tile, :], raw_ref.at[tile, :])
    for copy in leavings:
        copy.wait()


def embed(features, head, partner, cuts):
    outs = [jax.ShapeDtypeStruct((ROWS, E), F32)]
    outs += [jax.ShapeDtypeStruct((size + CODE, E), BF16) for _, size in cuts]
    hbm = pl.BlockSpec(memory_space=pltpu.HBM)
    tiles = ROWS // EMBED_TILE
    held = sum(max(size // EMBED_TILE, 1) for _, size in cuts)
    return pl.pallas_call(
        functools.partial(embed_kernel, cuts),
        out_shape=outs,
        in_specs=[hbm, hbm, hbm],
        out_specs=[hbm] * len(outs),
        scratch_shapes=[
            pltpu.VMEM(features.shape, BF16),
            pltpu.VMEM(head.shape, BF16),
            pltpu.VMEM((8, 128), jnp.int32),
            pltpu.VMEM((ROWS, E), F32),
            pltpu.VMEM((ROWS, E), BF16),
            pltpu.VMEM((len(cuts), CODE, E), BF16),
            pltpu.SemaphoreType.DMA((tiles + 2,)),
            pltpu.SemaphoreType.DMA((len(cuts) + held + tiles,)),
        ],
        compiler_params=pltpu.CompilerParams(vmem_limit_bytes=EMBED_LIMIT),
        cost_estimate=pl.CostEstimate(
            flops=2 * ROWS * 1024 * E, bytes_accessed=4 * 2**20, transcendentals=0
        ),
    )(features, head, partner.reshape(8, 128))


def tile_of(parts, at):
    size = parts[0].shape[0] - CODE
    return parts[at // size][at % size : at % size + TILE, :]


def term(rows, cols_ref, total, found, same_at=None):
    weight = 20.0 / total
    slope = 10.0 * math.log2(math.e)
    shift = slope - math.log2(weight)
    size = cols_ref.shape[0] - CODE
    cols = cols_ref[0:size, :]
    for at in range(0, ROWS, TILE):
        scores = lax.dot_general(tile_of(rows, at), cols, BOTH_LAST, preferred_element_type=F32)
        coef = 1.0 / (jnp.exp2(shift - scores * slope) + 1.0 / weight)
        if same_at is not None:
            i = lax.broadcasted_iota(jnp.int32, (TILE, size), 0) + at
            j = lax.broadcasted_iota(jnp.int32, (TILE, size), 1) + same_at
            coef = jnp.where(i != j, coef, 0.0)
        else:
            coef = coef.astype(BF16)
            coef = jnp.where(found(at), coef - jnp.bfloat16(weight), coef)
        yield slice(at, at + TILE), jnp.dot(coef.astype(BF16), cols, preferred_element_type=F32)


def matcher(spread_ref, place, row_first, cols_ref, col_first, col_at):
    ids = partners(cols_ref)
    col_partner = jnp.concatenate([ids[k : k + 1, :] for k in range(ids.shape[0])], axis=1)
    size = col_partner.shape[1]
    wide = size // 128

    def small(local, end):
        return jnp.clip(local, -1.0, float(end)).astype(jnp.int32).astype(jnp.int16)

    col_partner = col_partner - jnp.tile(row_first, (1, wide))
    col_partner = small(jnp.broadcast_to(col_partner, (16, size)), ROWS)
    col_partner = jnp.tile(col_partner, (TILE // 16, 1))
    col_ids = lax.broadcasted_iota(jnp.int32, (16, size), 1).astype(jnp.int16)
    col_ids = jnp.tile(col_ids, (TILE // 16, 1))

    def found(at):
        row_ids = (lax.broadcasted_iota(jnp.int32, (TILE, 128), 0) + at).astype(jnp.int16)
        theirs = spread_ref[place * ROWS + at : place * ROWS + at + TILE, :]
        theirs = small(theirs - (col_first + float(col_at)), size)
        return (jnp.tile(theirs, (1, wide)) == col_ids) | (
            col_partner == jnp.tile(row_ids, (1, wide))
        )

    return found


def diagonal_kernel(total, *refs):
    mine, grad_ref = refs[:-1], refs[-1]
    size = mine[0].shape[0] - CODE
    for k, part in enumerate(mine):
        for tile, value in term(mine, part, total, None, same_at=k * size):
            grad_ref[tile, :] = value if k == 0 else grad_ref[tile, :] + value


def chip_kernel(total, n_mine, first_ref, *refs):
    mine, other = refs[:n_mine], refs[n_mine:-4]
    grad_ref, new_ref, spread_ref, again_ref = refs[-4:]
    again_ref[...] = other[-1][...]
    for base, parts in ((0, mine), (ROWS, other)):
        at = base
        for part in parts:
            ids = partners(part)
            for k in range(ids.shape[0]):
                spread_ref[at : at + 128, :] = jnp.broadcast_to(ids[k : k + 1, :], (128, 128)).T
                at += 128
    size = other[0].shape[0] - CODE
    for k, part in enumerate(other):
        found = matcher(spread_ref, 0, first_ref[0:1, :], part, first_ref[1:2, :], k * size)
        old_ref = grad_ref if k == 0 else new_ref
        for tile, value in term(mine, part, total, found):
            new_ref[tile, :] = old_ref[tile, :] + value


def hold_kernel(cols_ref, after_ref, out_ref):
    out_ref[...] = cols_ref[...]


def rows_kernel(total, which, ats, jobs, outs, first_ref, spread_ref, *refs):
    refs = list(refs)
    news = refs[len(refs) - outs :]
    columns, refs = refs[: len(ats)], refs[len(ats) :]
    for (place, count, summed), new_ref in zip(jobs, news):
        rows, refs = refs[:count], refs[count:]
        old_ref = refs.pop(0) if summed else None
        row_first, col_first = first_ref[place : place + 1, :], first_ref[which : which + 1, :]
        works = []
        for cols_ref, at in zip(columns, ats):
            found = matcher(spread_ref, place, row_first, cols_ref, col_first, at)
            works.append(term(rows, cols_ref, total, found))
        for values in zip(*works):
            tile = values[0][0]
            value = sum(x for _, x in values)
            if old_ref is not None:
                value = old_ref[tile, :].astype(F32) + value
            new_ref[tile, :] = value.astype(new_ref.dtype)


def final_kernel(features_ref, raw_ref, grad_ref, extra_ref, raw_grad_ref, partial_ref):
    summed = None
    for at in range(0, ROWS, FINAL_TILE):
        tile = slice(at, at + FINAL_TILE)
        raw = raw_ref[tile, :]
        grad = grad_ref[tile, :] + extra_ref[tile, :].astype(F32)
        scale = lax.rsqrt(jnp.sum(raw * raw, axis=1, keepdims=True) + 1e-06)
        unit = raw * scale
        along = jnp.sum(unit * grad, axis=1, keepdims=True)
        raw_grad = ((grad - unit * along) * scale).astype(BF16)
        raw_grad_ref[tile, :] = raw_grad
        value = lax.dot_general(
            features_ref[tile, :], raw_grad, BOTH_FIRST, preferred_element_type=F32
        )
        summed = value if summed is None else summed + value
    partial_ref[...] = summed.astype(BF16)


def feature_kernel(raw_grad_ref, head_ref, out_ref):
    out_ref[...] = lax.dot_general(
        raw_grad_ref[...], head_ref[...], BOTH_LAST, preferred_element_type=F32
    ).astype(BF16)


def per_device(features, head, partner):
    count = lax.axis_size("batch")
    owner = lax.axis_index("batch")
    total = float(ROWS * count)
    pair = 4 * ROWS * ROWS * E
    shape = jax.ShapeDtypeStruct
    full = shape((ROWS, E), F32)

    def across_chip(x):
        return lax.ppermute(x, "batch", [(i, i ^ 1) for i in range(count)])

    def onward(x):
        hops = [(i, (i + (2 if i % 2 == 0 else -2)) % count) for i in range(count)]
        return lax.ppermute(x, "batch", hops)

    core = owner % 2
    chip = owner // 2
    back = jnp.where(core == 0, -1, 1)
    near = (chip + back) % (count // 2)
    far = (chip + 2 * back) % (count // 2)
    first_ids = jnp.stack(
        [
            owner,
            owner ^ 1,
            2 * near + core,
            2 * near + 1 - core,
            2 * far + core,
            2 * far + 1 - core,
            owner,
            owner,
        ]
    )
    first_ids = jnp.broadcast_to((first_ids * ROWS).astype(F32)[:, None], (8, 128))

    def cut(n):
        return [(k * ROWS // n, ROWS // n) for k in range(n)]

    if SAME_PARTS == CROSS_PARTS:
        raw, *mine = embed(features, head, partner, cut(SAME_PARTS))
        given_over = mine
    else:
        raw, *parts = embed(features, head, partner, cut(SAME_PARTS) + cut(CROSS_PARTS))
        mine, given_over = parts[:SAME_PARTS], parts[SAME_PARTS:]
    near_same = [onward(x) for x in mine]
    other = [across_chip(x) for x in given_over]

    grad = call(functools.partial(diagonal_kernel, total), full, [VMEM] * len(mine), OWN_COST * pair)(*mine)
    grad, spread, again = call(
        functools.partial(chip_kernel, total, len(mine)),
        (full, shape((2 * ROWS, 128), F32), shape(other[-1].shape, BF16)),
        [VMEM] + [VMEM] * (len(mine) + len(other) + 1),
        OWN_COST * pair,
    )(first_ids, *mine, *other, grad)
    near_cross = [onward(x) for x in other[:-1] + [again]]
    far_same = [onward(x) for x in near_same]

    def on_rows(which, ats, cols, jobs, outs, passed=None, after=()):
        given, plan = [], []
        for rows, old in jobs:
            plan.append((0 if rows is mine else 1, len(rows), old is not None))
            given += list(rows) + ([] if old is None else [old])
        tied = [] if passed is None else [passed]
        return call(
            functools.partial(rows_kernel, total, which, tuple(ats), tuple(plan), len(outs) + len(tied)),
            tuple(outs) + tuple(shape(x.shape, x.dtype) for x in tied),
            [VMEM] * (2 + len(cols) + len(given)) + [ANY] * (len(tied) + len(after)),
            len(jobs) * pair * sum(x.shape[0] - CODE for x in cols) // ROWS,
            {2 + len(cols) + len(given): len(outs)} if tied else {},
        )(first_ids, spread, *cols, *given, *tied, *after)

    theirs = None
    near = [(2, k * ROWS // len(near_same), x) for k, x in enumerate(near_same)]
    near += [(3, k * ROWS // len(near_cross), x) for k, x in enumerate(near_cross)]
    for k, (which, at, cols) in enumerate(near):
        after = [x for _, _, x in near[k + 1 : k + 2]] if k >= TIES else []
        theirs, grad = on_rows(
            which, [at], [cols], [(other, theirs), (mine, grad)], [full, full], after=after
        )
        if k == len(near_same) - 1:
            last = call(hold_kernel, shape(near_cross[-1].shape, BF16), [VMEM, ANY], 0)(
                near_cross[-1], grad
            )
            far_cross = [onward(x) for x in near_cross[:-1] + [last]]
    ats = [k * ROWS // len(far_same) for k in range(len(far_same))]
    grad, theirs = on_rows(4, ats, far_same, [(mine, grad)], [full], theirs)
    for k, cols in enumerate(far_cross[:-1]):
        theirs, grad = on_rows(
            5, [k * ROWS // len(far_cross)], [cols], [(other, theirs), (mine, grad)], [full, full]
        )
    last_at = ROWS - ROWS // len(far_cross)
    cols = far_cross[-1]
    (theirs,) = on_rows(5, [last_at], [cols], [(other, theirs)], [shape((ROWS, E), BF16)])
    extra = across_chip(theirs)
    (grad,) = on_rows(5, [last_at], [cols], [(mine, grad)], [full])

    raw_grad, partial = call(
        final_kernel,
        (shape((ROWS, E), BF16), shape((features.shape[1], E), BF16)),
        [VMEM] * 4,
        pair // 2,
    )(features, raw, grad, extra)
    parts = lax.all_to_all(partial.reshape(count, -1, E), "batch", 0, 0)
    feature_grad = call(
        feature_kernel, shape((ROWS, features.shape[1]), BF16), [VMEM] * 2, pair // 2
    )(raw_grad, head)
    head_grad = jnp.sum(parts.astype(F32), axis=0)
    return (feature_grad, head_grad)


def solution(mesh):
    in_specs = (P("batch", None), P(), P("batch"))
    out_specs = (P("batch", None), P("batch", None))
    return jax.shard_map(
        per_device, mesh=mesh, in_specs=in_specs, out_specs=out_specs, check_vma=False
    )
```

```python
import functools
import math

import jax
import jax.numpy as jnp
from jax import lax
from jax.experimental import pallas as pl
from jax.experimental.pallas import tpu as pltpu
from jax.sharding import PartitionSpec as P

BF16, F32 = jnp.bfloat16, jnp.float32
ROWS, E, CODE = 1024, 256, 16
TILE = 512
VMEM = pl.BlockSpec(memory_space=pltpu.VMEM)
ANY = pl.BlockSpec(memory_space=pl.ANY)
BOTH_LAST = (((1,), (1,)), ((), ()))
BOTH_FIRST = (((0,), (0,)), ((), ()))
LIMIT = 24 * 2**20
EMBED_LIMIT = 60 * 2**20
COST = 1
OWN_COST = 0.3
EMBED_TILE = 1024
SAME_PARTS, CROSS_PARTS = 2, 2
TIES = 1


def call(body, outs, specs, flops, aliases=None):
    return pl.pallas_call(
        body,
        out_shape=outs,
        in_specs=specs,
        out_specs=jax.tree.map(lambda _: VMEM, outs) if not aliases else (VMEM, ANY),
        input_output_aliases=aliases or {},
        compiler_params=pltpu.CompilerParams(vmem_limit_bytes=LIMIT),
        cost_estimate=pl.CostEstimate(flops=int(COST * flops), bytes_accessed=4 * 2**20, transcendentals=0),
    )


def partners(part_ref):
    size = part_ref.shape[0] - CODE
    code = part_ref[size : size + CODE, :].astype(F32)
    lines = size // 128
    return code[0:lines, 0:128] * 512.0 + code[0:lines, 128:256]


def embed_kernel(cuts, features_ref, head_ref, partner_ref, *refs):
    raw_ref, parts = refs[0], refs[1 : 1 + len(cuts)]
    held, weights, ids_held, raw_held, unit_held, code_held, arrived, left = refs[1 + len(cuts) :]
    tiles = [slice(at, at + EMBED_TILE) for at in range(0, ROWS, EMBED_TILE)]
    arrivals = [
        pltpu.make_async_copy(partner_ref, ids_held, arrived.at[len(tiles) + 1]),
        pltpu.make_async_copy(head_ref, weights, arrived.at[len(tiles)]),
    ]
    for k, tile in enumerate(tiles):
        arrivals.append(
            pltpu.make_async_copy(features_ref.at[tile, :], held.at[tile, :], arrived.at[k])
        )
    for copy in arrivals:
        copy.start()
    leavings = []

    def leave(source, target):
        copy = pltpu.make_async_copy(source, target, left.at[len(leavings)])
        copy.start()
        leavings.append(copy)

    arrivals[0].wait()
    ids = ids_held[...]
    high = (ids + 256) >> 9
    low = ids - (high << 9)
    code = jnp.concatenate([high, low], axis=1).astype(F32)
    for k, ((at, size), ref) in enumerate(zip(cuts, parts)):
        lines = code[at // 128 : (at + size) // 128, :]
        blank = jnp.zeros((CODE - size // 128, E), F32)
        code_held[k] = jnp.concatenate([lines, blank], axis=0).astype(BF16)
        leave(code_held.at[k], ref.at[size : size + CODE, :])
    arrivals[1].wait()
    for copy, tile in zip(arrivals[2:], tiles):
        copy.wait()
        raw = jnp.dot(held[tile, :], weights[...], preferred_element_type=F32)
        scale = lax.rsqrt(jnp.sum(raw * raw, axis=1, keepdims=True) + 1e-06)
        unit_held[tile, :] = (raw * scale).astype(BF16)
        for (at, size), ref in zip(cuts, parts):
            low_at, high_at = max(at, tile.start), min(at + size, tile.stop)
            if low_at < high_at:
                leave(unit_held.at[low_at:high_at, :], ref.at[low_at - at : high_at - at, :])
        raw_held[tile, :] = raw
        leave(raw_held.at[tile, :], raw_ref.at[tile, :])
    for copy in leavings:
        copy.wait()


def embed(features, head, partner, cuts):
    outs = [jax.ShapeDtypeStruct((ROWS, E), F32)]
    outs += [jax.ShapeDtypeStruct((size + CODE, E), BF16) for _, size in cuts]
    hbm = pl.BlockSpec(memory_space=pltpu.HBM)
    tiles = ROWS // EMBED_TILE
    held = sum(max(size // EMBED_TILE, 1) for _, size in cuts)
    return pl.pallas_call(
        functools.partial(embed_kernel, cuts),
        out_shape=outs,
        in_specs=[hbm, hbm, hbm],
        out_specs=[hbm] * len(outs),
        scratch_shapes=[
            pltpu.VMEM(features.shape, BF16),
            pltpu.VMEM(head.shape, BF16),
            pltpu.VMEM((8, 128), jnp.int32),
            pltpu.VMEM((ROWS, E), F32),
            pltpu.VMEM((ROWS, E), BF16),
            pltpu.VMEM((len(cuts), CODE, E), BF16),
            pltpu.SemaphoreType.DMA((tiles + 2,)),
            pltpu.SemaphoreType.DMA((len(cuts) + held + tiles,)),
        ],
        compiler_params=pltpu.CompilerParams(vmem_limit_bytes=EMBED_LIMIT),
        cost_estimate=pl.CostEstimate(
            flops=2 * ROWS * 1024 * E, bytes_accessed=4 * 2**20, transcendentals=0
        ),
    )(features, head, partner.reshape(8, 128))


def tile_of(parts, at):
    size = parts[0].shape[0] - CODE
    return parts[at // size][at % size : at % size + TILE, :]


def term(rows, cols_ref, total, found, same_at=None):
    weight = 20.0 / total
    slope = 10.0 * math.log2(math.e)
    shift = slope - math.log2(weight)
    size = cols_ref.shape[0] - CODE
    cols = cols_ref[0:size, :]
    for at in range(0, ROWS, TILE):
        scores = lax.dot_general(tile_of(rows, at), cols, BOTH_LAST, preferred_element_type=F32)
        coef = 1.0 / (jnp.exp2(shift - scores * slope) + 1.0 / weight)
        if same_at is not None:
            i = lax.broadcasted_iota(jnp.int32, (TILE, size), 0) + at
            j = lax.broadcasted_iota(jnp.int32, (TILE, size), 1) + same_at
            coef = jnp.where(i != j, coef, 0.0)
        else:
            coef = coef.astype(BF16)
            coef = jnp.where(found(at), coef - jnp.bfloat16(weight), coef)
        yield slice(at, at + TILE), jnp.dot(coef.astype(BF16), cols, preferred_element_type=F32)


def matcher(spread_ref, place, row_first, cols_ref, col_first, col_at):
    ids = partners(cols_ref)
    col_partner = jnp.concatenate([ids[k : k + 1, :] for k in range(ids.shape[0])], axis=1)
    size = col_partner.shape[1]
    wide = size // 128

    def small(local, end):
        return jnp.clip(local, -1.0, float(end)).astype(jnp.int32).astype(jnp.int16)

    col_partner = col_partner - jnp.tile(row_first, (1, wide))
    col_partner = small(jnp.broadcast_to(col_partner, (16, size)), ROWS)
    col_partner = jnp.tile(col_partner, (TILE // 16, 1))
    col_ids = lax.broadcasted_iota(jnp.int32, (16, size), 1).astype(jnp.int16)
    col_ids = jnp.tile(col_ids, (TILE // 16, 1))

    def found(at):
        row_ids = (lax.broadcasted_iota(jnp.int32, (TILE, 128), 0) + at).astype(jnp.int16)
        theirs = spread_ref[place * ROWS + at : place * ROWS + at + TILE, :]
        theirs = small(theirs - (col_first + float(col_at)), size)
        return (jnp.tile(theirs, (1, wide)) == col_ids) | (
            col_partner == jnp.tile(row_ids, (1, wide))
        )

    return found


def diagonal_kernel(total, *refs):
    mine, grad_ref = refs[:-1], refs[-1]
    size = mine[0].shape[0] - CODE
    for k, part in enumerate(mine):
        for tile, value in term(mine, part, total, None, same_at=k * size):
            grad_ref[tile, :] = value if k == 0 else grad_ref[tile, :] + value


def chip_kernel(total, n_mine, first_ref, *refs):
    mine, other = refs[:n_mine], refs[n_mine:-4]
    grad_ref, new_ref, spread_ref, again_ref = refs[-4:]
    again_ref[...] = other[-1][...]
    for base, parts in ((0, mine), (ROWS, other)):
        at = base
        for part in parts:
            ids = partners(part)
            for k in range(ids.shape[0]):
                spread_ref[at : at + 128, :] = jnp.broadcast_to(ids[k : k + 1, :], (128, 128)).T
                at += 128
    size = other[0].shape[0] - CODE
    for k, part in enumerate(other):
        found = matcher(spread_ref, 0, first_ref[0:1, :], part, first_ref[1:2, :], k * size)
        old_ref = grad_ref if k == 0 else new_ref
        for tile, value in term(mine, part, total, found):
            new_ref[tile, :] = old_ref[tile, :] + value


def rows_kernel(total, which, col_at, jobs, outs, first_ref, cols_ref, spread_ref, *refs):
    refs = list(refs)
    news = refs[len(refs) - outs :]
    for (place, count, summed), new_ref in zip(jobs, news):
        rows, refs = refs[:count], refs[count:]
        old_ref = refs.pop(0) if summed else None
        row_first, col_first = first_ref[place : place + 1, :], first_ref[which : which + 1, :]
        found = matcher(spread_ref, place, row_first, cols_ref, col_first, col_at)
        for tile, value in term(rows, cols_ref, total, found):
            if old_ref is not None:
                value = old_ref[tile, :].astype(F32) + value
            new_ref[tile, :] = value.astype(new_ref.dtype)


def final_kernel(features_ref, raw_ref, grad_ref, extra_ref, raw_grad_ref, partial_ref):
    raw = raw_ref[...]
    grad = grad_ref[...] + extra_ref[...].astype(F32)
    scale = lax.rsqrt(jnp.sum(raw * raw, axis=1, keepdims=True) + 1e-06)
    unit = raw * scale
    along = jnp.sum(unit * grad, axis=1, keepdims=True)
    raw_grad_ref[...] = ((grad - unit * along) * scale).astype(BF16)
    partial_ref[...] = lax.dot_general(
        features_ref[...], raw_grad_ref[...], BOTH_FIRST, preferred_element_type=F32
    ).astype(BF16)


def feature_kernel(raw_grad_ref, head_ref, out_ref):
    out_ref[...] = lax.dot_general(
        raw_grad_ref[...], head_ref[...], BOTH_LAST, preferred_element_type=F32
    ).astype(BF16)


def per_device(features, head, partner):
    count = lax.axis_size("batch")
    owner = lax.axis_index("batch")
    total = float(ROWS * count)
    pair = 4 * ROWS * ROWS * E
    shape = jax.ShapeDtypeStruct
    full = shape((ROWS, E), F32)

    def across_chip(x):
        return lax.ppermute(x, "batch", [(i, i ^ 1) for i in range(count)])

    def onward(x):
        hops = [(i, (i + (2 if i % 2 == 0 else -2)) % count) for i in range(count)]
        return lax.ppermute(x, "batch", hops)

    core = owner % 2
    chip = owner // 2
    back = jnp.where(core == 0, -1, 1)
    near = (chip + back) % (count // 2)
    far = (chip + 2 * back) % (count // 2)
    first_ids = jnp.stack(
        [
            owner,
            owner ^ 1,
            2 * near + core,
            2 * near + 1 - core,
            2 * far + core,
            2 * far + 1 - core,
            owner,
            owner,
        ]
    )
    first_ids = jnp.broadcast_to((first_ids * ROWS).astype(F32)[:, None], (8, 128))

    def cut(n):
        return [(k * ROWS // n, ROWS // n) for k in range(n)]

    if SAME_PARTS == CROSS_PARTS:
        raw, *mine = embed(features, head, partner, cut(SAME_PARTS))
        given_over = mine
    else:
        raw, *parts = embed(features, head, partner, cut(SAME_PARTS) + cut(CROSS_PARTS))
        mine, given_over = parts[:SAME_PARTS], parts[SAME_PARTS:]
    near_same = [onward(x) for x in mine]
    other = [across_chip(x) for x in given_over]

    grad = call(functools.partial(diagonal_kernel, total), full, [VMEM] * len(mine), OWN_COST * pair)(*mine)
    grad, spread, again = call(
        functools.partial(chip_kernel, total, len(mine)),
        (full, shape((2 * ROWS, 128), F32), shape(other[-1].shape, BF16)),
        [VMEM] + [VMEM] * (len(mine) + len(other) + 1),
        OWN_COST * pair,
    )(first_ids, *mine, *other, grad)
    near_cross = [onward(x) for x in other[:-1] + [again]]
    far_same = [onward(x) for x in near_same]
    far_cross = [onward(x) for x in near_cross]

    def on_rows(which, at, cols, jobs, outs, passed=None, after=()):
        given, plan = [], []
        for rows, old in jobs:
            plan.append((0 if rows is mine else 1, len(rows), old is not None))
            given += list(rows) + ([] if old is None else [old])
        tied = [] if passed is None else [passed]
        return call(
            functools.partial(rows_kernel, total, which, at, tuple(plan), len(outs) + len(tied)),
            tuple(outs) + tuple(shape(x.shape, x.dtype) for x in tied),
            [VMEM] + [VMEM] * (2 + len(given)) + [ANY] * (len(tied) + len(after)),
            len(jobs) * pair * (cols.shape[0] - CODE) // ROWS,
            {3 + len(given): len(outs)} if tied else {},
        )(first_ids, cols, spread, *given, *tied, *after)

    theirs = None
    near = [(2, k * ROWS // len(near_same), x) for k, x in enumerate(near_same)]
    near += [(3, k * ROWS // len(near_cross), x) for k, x in enumerate(near_cross)]
    for k, (which, at, cols) in enumerate(near):
        after = [x for _, _, x in near[k + 1 : k + 2]] if k >= TIES else []
        theirs, grad = on_rows(
            which, at, cols, [(other, theirs), (mine, grad)], [full, full], after=after
        )
    for k, cols in enumerate(far_same):
        grad, theirs = on_rows(4, k * ROWS // len(far_same), cols, [(mine, grad)], [full], theirs)
    for k, cols in enumerate(far_cross[:-1]):
        theirs, grad = on_rows(
            5, k * ROWS // len(far_cross), cols, [(other, theirs), (mine, grad)], [full, full]
        )
    last_at = ROWS - ROWS // len(far_cross)
    cols = far_cross[-1]
    (theirs,) = on_rows(5, last_at, cols, [(other, theirs)], [shape((ROWS, E), BF16)])
    extra = across_chip(theirs)
    (grad,) = on_rows(5, last_at, cols, [(mine, grad)], [full])

    raw_grad, partial = call(
        final_kernel,
        (shape((ROWS, E), BF16), shape((features.shape[1], E), BF16)),
        [VMEM] * 4,
        pair // 2,
    )(features, raw, grad, extra)
    parts = lax.all_to_all(partial.reshape(count, -1, E), "batch", 0, 0)
    feature_grad = call(
        feature_kernel, shape((ROWS, features.shape[1]), BF16), [VMEM] * 2, pair // 2
    )(raw_grad, head)
    head_grad = jnp.sum(parts.astype(F32), axis=0)
    return (feature_grad, head_grad)


def solution(mesh):
    in_specs = (P("batch", None), P(), P("batch"))
    out_specs = (P("batch", None), P("batch", None))
    return jax.shard_map(
        per_device, mesh=mesh, in_specs=in_specs, out_specs=out_specs, check_vma=False
    )
```
